32 devices in a mesh: tm: 4 (over y, x), stat: 8 (over z, core).
Axes of the slice: x: 2, y: 2, z: 4, core: 2. Of those that a mesh axis runs over, the one named last changes fastest.
Arguments:
- voltages: bfloat16 [512, 163840], P('stat', 'tm'), may hold values from -6 to 6
- taper: float32 [16, 4096], replicated, may hold values from -1.5 to 1.5
Outputs:
- visibility: float32 [4, 2, 512, 5, 64, 512], P('tm', None, 'stat')
The draws below stay inside these ranges and needn't reach their ends.
All inputs are finite; a program needn't handle non-finite values.
Results may differ from the reference program's by a relative error of at most 0.0039.
Values may be sent and summed in bfloat16 or wider, within the bound.
A program may use at most 512 MiB of HBM per device.

```python
import math
import jax
import jax.numpy as jnp
from jax import lax

CHANNELS = 2048
TAPS = 16
NSPEC = 25
INPUTS = 512
FRAME = 4096
SAMPLES = 163840
IN_DEV = 64
CH_DEV = 512
LAGS = 5
N_TM = 4
N_STAT = 8


def block_scale(own_key, dims, pieces, smallest, high):
    def one(dim, blocks):
        steps = jax.random.uniform(jax.random.fold_in(jax.random.fold_in(own_key, 6), dim), (blocks,), jnp.float32, smallest / len(pieces), high / len(pieces))
        return jnp.repeat(jnp.exp(steps), dims[dim] // blocks).reshape((-1,) + (1,) * (len(dims) - dim - 1))

    factor_of = one(*pieces[0])
    for cut in pieces[1:]:
        factor_of = factor_of * one(*cut)
    return factor_of


def centred(stream_key, dims, width, limit, shards=(), held_as=jnp.bfloat16):
    values = width * jax.random.normal(stream_key, dims, jnp.float32)
    if shards:
        values = values * block_scale(stream_key, dims, shards, -0.22, 0.18)
    return jnp.clip(values, -limit, limit).astype(held_as)


def setup_inputs(seed: int = 0) -> dict:
    seeds = jax.random.split(jax.random.key(seed), 3)
    return {
        "voltages": centred(seeds[0], (INPUTS, SAMPLES), 1.0, 6.0, ((0, 8), (1, 4))),
        "taper": centred(seeds[1], (TAPS, FRAME), TAPS ** -0.5, 1.5, (), jnp.float32),
    }


def reference(voltages, taper):
    frames = voltages.astype(jnp.float32).reshape(INPUTS, NSPEC + TAPS - 1, FRAME)
    filtered = jnp.zeros((INPUTS, NSPEC, FRAME), jnp.float32)
    for tap_index in range(TAPS):
        filtered = filtered + taper[tap_index][None, None, :] * frames[:, tap_index:tap_index + NSPEC, :]
    spectrum = jnp.fft.rfft(filtered, axis=-1)[..., :CHANNELS] / math.sqrt(FRAME)
    real_part = jnp.real(spectrum).astype(jnp.bfloat16).astype(jnp.float32)
    imag_part = jnp.imag(spectrum).astype(jnp.bfloat16).astype(jnp.float32)
    real_part = jnp.transpose(real_part.reshape(INPUTS, NSPEC, CH_DEV, N_TM), (3, 0, 1, 2))
    imag_part = jnp.transpose(imag_part.reshape(INPUTS, NSPEC, CH_DEV, N_TM), (3, 0, 1, 2))

    def residue_block(parts):
        group_real = parts[0].reshape(N_STAT, IN_DEV, NSPEC, CH_DEV)
        group_imag = parts[1].reshape(N_STAT, IN_DEV, NSPEC, CH_DEV)

        def one_lag(lag_index):
            other_real = jnp.roll(group_real, -lag_index, axis=0)
            other_imag = jnp.roll(group_imag, -lag_index, axis=0)
            cross_real = jnp.einsum('gisc,gmsc->gimc', group_real, other_real) + jnp.einsum('gisc,gmsc->gimc', group_imag, other_imag)
            cross_imag = jnp.einsum('gisc,gmsc->gimc', group_imag, other_real) - jnp.einsum('gisc,gmsc->gimc', group_real, other_imag)
            return jnp.stack([cross_real, cross_imag]) / NSPEC
        stacked = lax.map(one_lag, jnp.arange(LAGS, dtype=jnp.int32))
        stacked = jnp.transpose(stacked, (1, 2, 3, 0, 4, 5))
        return stacked.reshape(2, INPUTS, LAGS, IN_DEV, CH_DEV)
    return lax.map(residue_block, (real_part, imag_part))
```

```python
import math

import jax
import jax.numpy as jnp
import numpy as np
from jax import lax
from jax.experimental import pallas as pl
from jax.experimental.pallas import tpu as pltpu
from jax.sharding import PartitionSpec as P

NSPEC = 25
LANES = 128


def from_behind(value, axis, steps):
    count = lax.axis_size(axis)
    pairs = [(source, (source + steps) % count) for source in range(count)]
    return lax.ppermute(value, axis, pairs)


def dft_table(segment, channel_count, frame_len):
    sample_idx = np.arange(segment, dtype=np.int64)[:, None]
    channel_idx = np.arange(channel_count, dtype=np.int64)[None, :]
    angles = 2.0 * math.pi / segment * (sample_idx * channel_idx % segment)
    cosine, sine = np.cos(angles), np.sin(angles)
    upper = np.concatenate([cosine, -sine], axis=1)
    lower = np.concatenate([sine, cosine], axis=1)
    table = np.concatenate([upper, lower], axis=0) / math.sqrt(frame_len)
    return table.astype(np.float32)


def fold_twiddle(filtered, tm_count, frame_len):
    row_count = filtered.shape[0]
    segment = frame_len // tm_count
    pieces = filtered.reshape(row_count, tm_count, segment)
    blocks = []
    for residue in range(tm_count):
        outer = 2.0 * math.pi / tm_count * (residue * np.arange(tm_count) % tm_count)
        inner = 2.0 * math.pi / frame_len * (residue * np.arange(segment) % frame_len)
        inner_cos = np.cos(inner).astype(np.float32)[None, :]
        inner_sin = np.sin(inner).astype(np.float32)[None, :]
        sum_real = sum(float(np.round(np.cos(a), 15)) * pieces[:, n] for n, a in enumerate(outer))
        sum_imag = sum(float(np.round(-np.sin(a), 15)) * pieces[:, n] for n, a in enumerate(outer))
        twisted_real = sum_real * inner_cos + sum_imag * inner_sin
        twisted_imag = sum_imag * inner_cos - sum_real * inner_sin
        blocks.append(jnp.concatenate([twisted_real, twisted_imag], axis=1))
    return jnp.stack(blocks)


def polyphase(series, taper, spectra_count):
    row_count = series.shape[0]
    tap_count, frame_len = taper.shape
    frames = series.reshape(row_count, spectra_count + tap_count - 1, frame_len)
    frames = jnp.transpose(frames, (1, 0, 2))
    filtered = jnp.zeros((spectra_count, row_count, frame_len), jnp.float32)
    for tap_index in range(tap_count):
        filtered = filtered + taper[tap_index][None, None, :] * frames[
            tap_index : tap_index + spectra_count
        ].astype(jnp.float32)
    return filtered


def correlate_kernel(inputs, channels, own_ref, partner_ref, *rest):
    out_ref, products = rest[-2], rest[-1]
    scale = jnp.float32(1.0 / NSPEC)

    def multiply(c, carry):
        products[pl.ds(c * inputs, inputs), :] = (
            jnp.dot(own_ref[c], partner_ref[c], preferred_element_type=jnp.float32) * scale
        )
        return carry

    lax.fori_loop(0, channels, multiply, 0, unroll=8)

    def turn(i, carry):
        tile = jnp.transpose(products[pl.ds(i, channels, stride=inputs), :])
        out_ref[0, i, 0] = tile[:inputs]
        out_ref[1, i, 0] = tile[inputs:]
        return carry

    lax.fori_loop(0, inputs, turn, 0, unroll=4)


def correlate(own, partner, visibility, lag, lag_count):
    channel_count, inputs, depth = own.shape
    block = min(LANES, channel_count)
    out_shape = (2, inputs, lag_count, inputs, channel_count)
    in_specs = [
        pl.BlockSpec((block, inputs, depth), lambda c: (c, 0, 0)),
        pl.BlockSpec((block, depth, 2 * inputs), lambda c: (c, 0, 0)),
    ]
    operands = [own, partner]
    aliases = {}
    if visibility is not None:
        in_specs.append(pl.BlockSpec(memory_space=pl.ANY))
        operands.append(visibility)
        aliases = {2: 0}

    def kernel(*refs):
        correlate_kernel(inputs, block, *refs)

    return pl.pallas_call(
        kernel,
        grid=(channel_count // block,),
        out_shape=jax.ShapeDtypeStruct(out_shape, jnp.float32),
        in_specs=in_specs,
        out_specs=pl.BlockSpec((2, inputs, 1, inputs, block), lambda c: (0, 0, lag, 0, c)),
        scratch_shapes=[pltpu.VMEM((block * inputs, 2 * inputs), jnp.float32)],
        input_output_aliases=aliases,
        compiler_params=pltpu.CompilerParams(vmem_limit_bytes=40 * 1024 * 1024),
        cost_estimate=pl.CostEstimate(
            flops=50_000_000_000, bytes_accessed=32_000_000, transcendentals=0
        ),
    )(*operands)


def pad_depth(value, axis, depth):
    widths = [(0, 0)] * value.ndim
    widths[axis] = (0, depth - value.shape[axis])
    return jnp.pad(value, widths)


def partner_form(block, depth):
    real, imag = block[:, :, 0], block[:, :, 1]
    upper = jnp.concatenate([real, -imag], axis=-1)
    lower = jnp.concatenate([imag, real], axis=-1)
    both = jnp.concatenate([pad_depth(upper, 0, depth), pad_depth(lower, 0, depth)], axis=0)
    return jnp.transpose(both, (1, 0, 2))


def shards(voltages, taper):
    tm_count = lax.axis_size("tm")
    stat_count = lax.axis_size("stat")
    local_inputs = voltages.shape[0]
    frame_len = taper.shape[1]
    segment = frame_len // tm_count
    channel_count = frame_len // 2 // tm_count
    lag_count = stat_count // 2 + 1
    per = local_inputs // tm_count
    depth = 32
    table = dft_table(segment, channel_count, frame_len)

    series = lax.all_to_all(voltages, "tm", split_axis=0, concat_axis=1, tiled=True)
    filtered = polyphase(series, taper, NSPEC)
    twisted = fold_twiddle(filtered.reshape(NSPEC * per, frame_len), tm_count, frame_len)
    spectra = jnp.dot(
        twisted.reshape(tm_count * NSPEC * per, 2 * segment),
        table,
        precision=lax.Precision.HIGH,
        preferred_element_type=jnp.float32,
    ).astype(jnp.bfloat16)
    spectra = spectra.reshape(tm_count, NSPEC * per, 2 * channel_count)
    spectra = lax.all_to_all(spectra, "tm", split_axis=0, concat_axis=0, tiled=True)
    spectra = spectra.reshape(tm_count, NSPEC, per, 2, channel_count)
    block = jnp.transpose(spectra, (1, 4, 3, 0, 2)).reshape(
        NSPEC, channel_count, 2 * local_inputs
    )
    unpacked = block.reshape(NSPEC, channel_count, 2, local_inputs)
    own = jnp.transpose(pad_depth(unpacked, 0, depth), (1, 3, 2, 0)).reshape(
        channel_count, local_inputs, 2 * depth
    )
    visibility = None
    for lag in range(lag_count):
        following = from_behind(block, "stat", -1) if lag < lag_count - 1 else None
        partner = partner_form(
            block.reshape(NSPEC, channel_count, 2, local_inputs), depth
        )
        visibility = correlate(own, partner, visibility, lag, lag_count)
        block = following
    return visibility[None]


def solution(mesh):
    return jax.shard_map(
        shards,
        mesh=mesh,
        in_specs=(P("stat", "tm"), P()),
        out_specs=P("tm", None, "stat", None, None, None),
        check_vma=False,
    )
```

```python
import math

import jax
import jax.numpy as jnp
import numpy as np
from jax import lax
from jax.experimental import pallas as pl
from jax.experimental.pallas import tpu as pltpu
from jax.sharding import PartitionSpec as P

NSPEC = 25
LANES = 128
DEPTH = 32


def from_behind(value, axis, steps):
    count = lax.axis_size(axis)
    pairs = [(source, (source + steps) % count) for source in range(count)]
    return lax.ppermute(value, axis, pairs)


def dft_table(segment, channel_count, frame_len, width):
    sample_idx = np.arange(segment, dtype=np.int64)[:, None]
    channel_idx = np.arange(channel_count, dtype=np.int64)[None, :]
    angles = 2.0 * math.pi / segment * (sample_idx * channel_idx % segment)
    cosine, sine = np.cos(angles), np.sin(angles)
    upper = np.concatenate([cosine, -sine], axis=1)
    lower = np.concatenate([sine, cosine], axis=1)
    table = np.stack([upper, lower]) / math.sqrt(frame_len)
    table = table.reshape(2, segment // width, width, 2 * channel_count)
    return table.transpose(1, 0, 2, 3).reshape(2 * segment, 2 * channel_count).astype(np.float32)


def twiddle_tables(tm_count, frame_len):
    segment = frame_len // tm_count
    turns = np.arange(tm_count)[:, None] * np.arange(segment)[None, :] % frame_len
    angles = 2.0 * math.pi / frame_len * turns
    return np.cos(angles).astype(np.float32), np.sin(angles).astype(np.float32)


def weighted(pieces, weights):
    total = None
    for piece, weight in zip(pieces, weights):
        weight = float(np.round(weight, 15))
        if weight == 0.0:
            continue
        term = piece if weight == 1.0 else (-piece if weight == -1.0 else piece * weight)
        total = term if total is None else total + term
    return jnp.zeros_like(pieces[0]) if total is None else total


def channelize_kernel(tm_count, width, series_ref, taper_ref, cos_ref, sin_ref, out_ref, frames):
    tap_count, frame_len = taper_ref.shape
    segment = frame_len // tm_count
    per_source = series_ref.shape[2] // frame_len
    start = pl.program_id(0) * width
    for source in range(tm_count):
        for frame in range(per_source):
            for outer in range(tm_count):
                column = pl.multiple_of(frame * frame_len + outer * segment + start, width)
                frames[source * per_source + frame, outer] = series_ref[
                    source, :, pl.ds(column, width)
                ].astype(jnp.float32)

    def spectrum(s, carry):
        pieces = []
        for outer in range(tm_count):
            column = pl.multiple_of(outer * segment + start, width)
            total = None
            for tap in range(tap_count):
                term = taper_ref[tap : tap + 1, pl.ds(column, width)] * frames[s + tap, outer]
                total = term if total is None else total + term
            pieces.append(total)
        for residue in range(tm_count):
            angles = 2.0 * math.pi / tm_count * (residue * np.arange(tm_count) % tm_count)
            sum_real = weighted(pieces, np.cos(angles))
            sum_imag = weighted(pieces, -np.sin(angles))
            inner_cos = cos_ref[residue : residue + 1, :]
            inner_sin = sin_ref[residue : residue + 1, :]
            out_ref[residue, s, :, :width] = sum_real * inner_cos + sum_imag * inner_sin
            out_ref[residue, s, :, width:] = sum_imag * inner_cos - sum_real * inner_sin
        return carry

    lax.fori_loop(0, NSPEC, spectrum, 0)


def channelize(series, taper, width):
    tm_count, inputs, samples = series.shape
    tap_count, frame_len = taper.shape
    segment = frame_len // tm_count
    inner_cos, inner_sin = twiddle_tables(tm_count, frame_len)
    frame_count = tm_count * samples // frame_len

    def kernel(*refs):
        channelize_kernel(tm_count, width, *refs)

    return pl.pallas_call(
        kernel,
        grid=(segment // width,),
        out_shape=jax.ShapeDtypeStruct((tm_count, NSPEC, inputs, 2 * segment), jnp.float32),
        in_specs=[
            pl.BlockSpec(series.shape, lambda n: (0, 0, 0)),
            pl.BlockSpec(taper.shape, lambda n: (0, 0)),
            pl.BlockSpec((tm_count, width), lambda n: (0, n)),
            pl.BlockSpec((tm_count, width), lambda n: (0, n)),
        ],
        out_specs=pl.BlockSpec((tm_count, NSPEC, inputs, 2 * width), lambda n: (0, 0, 0, n)),
        scratch_shapes=[pltpu.VMEM((frame_count, tm_count, inputs, width), jnp.float32)],
        compiler_params=pltpu.CompilerParams(vmem_limit_bytes=40 * 1024 * 1024),
        cost_estimate=pl.CostEstimate(
            flops=200_000_000, bytes_accessed=20_000_000, transcendentals=0
        ),
    )(series, taper, inner_cos, inner_sin)


def correlate_kernel(inputs, channels, first, *refs):
    if first:
        partner_ref, out_ref, own_ref, rows, products = refs
    else:
        own_ref, partner_ref, _, out_ref, rows, products = refs
    scale = jnp.float32(1.0 / NSPEC)
    lanes = 2 * inputs
    total = channels * NSPEC
    rows[pl.ds(0, total), :] = partner_ref[...].astype(jnp.float32)
    rows[pl.ds(total, 8), :] = jnp.zeros((8, lanes), jnp.float32)
    lane = lax.broadcasted_iota(jnp.int32, (DEPTH, lanes), 1)
    sign = jnp.where(lane < inputs, 1.0, -1.0).astype(jnp.float32)
    held = lax.broadcasted_iota(jnp.int32, (DEPTH, lanes), 0) < NSPEC

    def multiply(c, carry):
        both = rows[pl.ds(c * NSPEC, DEPTH), :]
        if lanes == LANES:
            swapped = pltpu.roll(both, inputs, 1)
        else:
            swapped = jnp.concatenate([both[:, inputs:], both[:, :inputs]], axis=1)
        right = jnp.concatenate([both * sign, swapped], axis=0).astype(jnp.bfloat16)
        if first:
            turned = jnp.transpose(jnp.where(held, both, 0.0))
            left = jnp.concatenate([turned[:inputs], turned[inputs:]], axis=1)
            left = left.astype(jnp.bfloat16)
            own_ref[c] = left
        else:
            left = own_ref[c]
        products[pl.ds(c * inputs, inputs), :] = (
            jnp.dot(left, right, preferred_element_type=jnp.float32) * scale
        )
        return carry

    lax.fori_loop(0, channels, multiply, 0, unroll=8)

    def turn(i, carry):
        tile = jnp.transpose(products[pl.ds(i, channels, stride=inputs), :])
        out_ref[0, i, 0] = tile[:inputs]
        out_ref[1, i, 0] = tile[inputs:]
        return carry

    lax.fori_loop(0, inputs, turn, 0, unroll=4)


def correlate(own, partner, visibility, lag, lag_count, inputs, channel_count):
    block = min(LANES, channel_count)
    out_shape = [
        jax.ShapeDtypeStruct((2, inputs, lag_count, inputs, channel_count), jnp.float32)
    ]
    out_specs = [pl.BlockSpec((2, inputs, 1, inputs, block), lambda c: (0, 0, lag, 0, c))]
    own_spec = pl.BlockSpec((block, inputs, 2 * DEPTH), lambda c: (c, 0, 0))
    partner_spec = pl.BlockSpec((block * NSPEC, 2 * inputs), lambda c: (c, 0))
    first = own is None
    if first:
        in_specs, operands, aliases = [partner_spec], [partner], {}
        out_shape.append(
            jax.ShapeDtypeStruct((channel_count, inputs, 2 * DEPTH), jnp.bfloat16)
        )
        out_specs.append(own_spec)
    else:
        in_specs = [own_spec, partner_spec, pl.BlockSpec(memory_space=pl.ANY)]
        operands, aliases = [own, partner, visibility], {2: 0}

    def kernel(*refs):
        correlate_kernel(inputs, block, first, *refs)

    results = pl.pallas_call(
        kernel,
        grid=(channel_count // block,),
        out_shape=out_shape,
        in_specs=in_specs,
        out_specs=out_specs,
        scratch_shapes=[
            pltpu.VMEM((block * NSPEC + 8, 2 * inputs), jnp.float32),
            pltpu.VMEM((block * inputs, 2 * inputs), jnp.float32),
        ],
        input_output_aliases=aliases,
        compiler_params=pltpu.CompilerParams(vmem_limit_bytes=40 * 1024 * 1024),
        cost_estimate=pl.CostEstimate(
            flops=35_000_000_000, bytes_accessed=24_000_000, transcendentals=0
        ),
    )(*operands)
    return (results[0], results[1]) if first else (results[0], own)


def shards(voltages, taper):
    tm_count = lax.axis_size("tm")
    stat_count = lax.axis_size("stat")
    local_inputs, samples = voltages.shape
    frame_len = taper.shape[1]
    segment = frame_len // tm_count
    channel_count = frame_len // 2 // tm_count
    lag_count = stat_count // 2 + 1
    per = local_inputs // tm_count
    table = dft_table(segment, channel_count, frame_len, LANES)

    series = lax.all_to_all(
        voltages.reshape(tm_count, per, samples), "tm", split_axis=0, concat_axis=0, tiled=True
    )
    twisted = channelize(series, taper, LANES)
    spectra = jnp.dot(
        twisted.reshape(tm_count * NSPEC * per, 2 * segment),
        table,
        precision=lax.Precision.HIGH,
        preferred_element_type=jnp.float32,
    ).astype(jnp.bfloat16)
    spectra = spectra.reshape(tm_count, NSPEC * per, 2 * channel_count)
    spectra = lax.all_to_all(spectra, "tm", split_axis=0, concat_axis=0, tiled=True)
    spectra = spectra.reshape(tm_count, NSPEC, per, 2, channel_count)
    block = jnp.transpose(spectra, (4, 1, 3, 0, 2)).reshape(
        channel_count * NSPEC, 2 * local_inputs
    )
    visibility = own = None
    for lag in range(lag_count):
        following = from_behind(block, "stat", -1) if lag < lag_count - 1 else None
        visibility, own = correlate(
            own, block, visibility, lag, lag_count, local_inputs, channel_count
        )
        block = following
    return visibility[None]


def solution(mesh):
    return jax.shard_map(
        shards,
        mesh=mesh,
        in_specs=(P("stat", "tm"), P()),
        out_specs=P("tm", None, "stat", None, None, None),
        check_vma=False,
    )
```

```python
import math

import jax
import jax.numpy as jnp
import numpy as np
from jax import lax
from jax.experimental import pallas as pl
from jax.experimental.pallas import tpu as pltpu
from jax.sharding import PartitionSpec as P

NSPEC = 25
LANES = 128
DEPTH = 32
PARTS = 2


def from_behind(value, axis, steps):
    count = lax.axis_size(axis)
    pairs = [(source, (source + steps) % count) for source in range(count)]
    return lax.ppermute(value, axis, pairs)


def dft_table(segment, channel_count, frame_len, width):
    sample_idx = np.arange(segment, dtype=np.int64)[:, None]
    channel_idx = np.arange(channel_count, dtype=np.int64)[None, :]
    angles = 2.0 * math.pi / segment * (sample_idx * channel_idx % segment)
    cosine, sine = np.cos(angles), np.sin(angles)
    upper = np.concatenate([cosine, -sine], axis=1)
    lower = np.concatenate([sine, cosine], axis=1)
    table = np.stack([upper, lower]) / math.sqrt(frame_len)
    table = table.reshape(2, segment // width, width, 2 * channel_count)
    return table.transpose(1, 0, 2, 3).reshape(2 * segment, 2 * channel_count).astype(np.float32)


def twiddle_tables(tm_count, frame_len):
    segment = frame_len // tm_count
    turns = np.arange(tm_count)[:, None] * np.arange(segment)[None, :] % frame_len
    angles = 2.0 * math.pi / frame_len * turns
    return np.cos(angles).astype(np.float32), np.sin(angles).astype(np.float32)


def weighted(pieces, weights):
    total = None
    for piece, weight in zip(pieces, weights):
        weight = float(np.round(weight, 15))
        if weight == 0.0:
            continue
        term = piece if weight == 1.0 else (-piece if weight == -1.0 else piece * weight)
        total = term if total is None else total + term
    return jnp.zeros_like(pieces[0]) if total is None else total


def channelize_kernel(tm_count, width, series_ref, taper_ref, cos_ref, sin_ref, out_ref, frames):
    tap_count, frame_len = taper_ref.shape
    segment = frame_len // tm_count
    per_source = series_ref.shape[2] // frame_len
    start = pl.program_id(0) * width
    for source in range(tm_count):
        for frame in range(per_source):
            for outer in range(tm_count):
                column = pl.multiple_of(frame * frame_len + outer * segment + start, width)
                frames[source * per_source + frame, outer] = series_ref[
                    source, :, pl.ds(column, width)
                ].astype(jnp.float32)

    def spectrum(s, carry):
        pieces = []
        for outer in range(tm_count):
            column = pl.multiple_of(outer * segment + start, width)
            total = None
            for tap in range(tap_count):
                term = taper_ref[tap : tap + 1, pl.ds(column, width)] * frames[s + tap, outer]
                total = term if total is None else total + term
            pieces.append(total)
        for residue in range(tm_count):
            angles = 2.0 * math.pi / tm_count * (residue * np.arange(tm_count) % tm_count)
            sum_real = weighted(pieces, np.cos(angles))
            sum_imag = weighted(pieces, -np.sin(angles))
            inner_cos = cos_ref[residue : residue + 1, :]
            inner_sin = sin_ref[residue : residue + 1, :]
            out_ref[residue, s, :, :width] = sum_real * inner_cos + sum_imag * inner_sin
            out_ref[residue, s, :, width:] = sum_imag * inner_cos - sum_real * inner_sin
        return carry

    lax.fori_loop(0, NSPEC, spectrum, 0)


def channelize(series, taper, width):
    tm_count, inputs, samples = series.shape
    tap_count, frame_len = taper.shape
    segment = frame_len // tm_count
    inner_cos, inner_sin = twiddle_tables(tm_count, frame_len)
    frame_count = tm_count * samples // frame_len

    def kernel(*refs):
        channelize_kernel(tm_count, width, *refs)

    return pl.pallas_call(
        kernel,
        grid=(segment // width,),
        out_shape=jax.ShapeDtypeStruct((tm_count, NSPEC, inputs, 2 * segment), jnp.float32),
        in_specs=[
            pl.BlockSpec(series.shape, lambda n: (0, 0, 0)),
            pl.BlockSpec(taper.shape, lambda n: (0, 0)),
            pl.BlockSpec((tm_count, width), lambda n: (0, n)),
            pl.BlockSpec((tm_count, width), lambda n: (0, n)),
        ],
        out_specs=pl.BlockSpec((tm_count, NSPEC, inputs, 2 * width), lambda n: (0, 0, 0, n)),
        scratch_shapes=[pltpu.VMEM((frame_count, tm_count, inputs, width), jnp.float32)],
        compiler_params=pltpu.CompilerParams(vmem_limit_bytes=40 * 1024 * 1024),
        cost_estimate=pl.CostEstimate(
            flops=200_000_000, bytes_accessed=20_000_000, transcendentals=0
        ),
    )(series, taper, inner_cos, inner_sin)


def correlate_kernel(inputs, channels, first, *refs):
    rows, products = refs[-2:]
    if first:
        partner_ref, out_ref, own_ref = refs[0], refs[-4], refs[-3]
    else:
        own_ref, partner_ref, out_ref = refs[0], refs[1], refs[-3]
    scale = jnp.float32(1.0 / NSPEC)
    lanes = 2 * inputs
    total = channels * NSPEC
    rows[pl.ds(0, total), :] = partner_ref[...].astype(jnp.float32)
    rows[pl.ds(total, 8), :] = jnp.zeros((8, lanes), jnp.float32)
    lane = lax.broadcasted_iota(jnp.int32, (DEPTH, lanes), 1)
    sign = jnp.where(lane < inputs, 1.0, -1.0).astype(jnp.float32)
    held = lax.broadcasted_iota(jnp.int32, (DEPTH, lanes), 0) < NSPEC

    def multiply(c, carry):
        both = rows[pl.ds(c * NSPEC, DEPTH), :]
        if lanes == LANES:
            swapped = pltpu.roll(both, inputs, 1)
        else:
            swapped = jnp.concatenate([both[:, inputs:], both[:, :inputs]], axis=1)
        right = jnp.concatenate([both * sign, swapped], axis=0).astype(jnp.bfloat16)
        if first:
            turned = jnp.transpose(jnp.where(held, both, 0.0))
            left = jnp.concatenate([turned[:inputs], turned[inputs:]], axis=1)
            left = left.astype(jnp.bfloat16)
            own_ref[c] = left
        else:
            left = own_ref[c]
        products[pl.ds(c * inputs, inputs), :] = (
            jnp.dot(left, right, preferred_element_type=jnp.float32) * scale
        )
        return carry

    lax.fori_loop(0, channels, multiply, 0, unroll=8)

    def turn(i, carry):
        tile = jnp.transpose(products[pl.ds(i, channels, stride=inputs), :])
        out_ref[0, i, 0] = tile[:inputs]
        out_ref[1, i, 0] = tile[inputs:]
        return carry

    lax.fori_loop(0, inputs, turn, 0, unroll=4)


def correlate(own, partner, visibility, lag, lag_count, inputs, channel_count, part, parts):
    part_channels = channel_count // parts
    block = min(LANES, part_channels)
    ahead = part * (part_channels // block)
    out_shape = [
        jax.ShapeDtypeStruct((2, inputs, lag_count, inputs, channel_count), jnp.float32)
    ]
    out_specs = [pl.BlockSpec((2, inputs, 1, inputs, block), lambda c: (0, 0, lag, 0, ahead + c))]
    own_spec = pl.BlockSpec((block, inputs, 2 * DEPTH), lambda c: (c, 0, 0))
    partner_spec = pl.BlockSpec((block * NSPEC, 2 * inputs), lambda c: (c, 0))
    first = own is None
    if first:
        in_specs, operands = [partner_spec], [partner]
        out_shape.append(
            jax.ShapeDtypeStruct((part_channels, inputs, 2 * DEPTH), jnp.bfloat16)
        )
        out_specs.append(own_spec)
    else:
        in_specs, operands = [own_spec, partner_spec], [own, partner]
    aliases = {}
    if visibility is not None:
        aliases = {len(operands): 0}
        in_specs.append(pl.BlockSpec(memory_space=pl.ANY))
        operands.append(visibility)

    def kernel(*refs):
        correlate_kernel(inputs, block, first, *refs)

    results = pl.pallas_call(
        kernel,
        grid=(part_channels // block,),
        out_shape=out_shape,
        in_specs=in_specs,
        out_specs=out_specs,
        scratch_shapes=[
            pltpu.VMEM((block * NSPEC + 8, 2 * inputs), jnp.float32),
            pltpu.VMEM((block * inputs, 2 * inputs), jnp.float32),
        ],
        input_output_aliases=aliases,
        compiler_params=pltpu.CompilerParams(vmem_limit_bytes=40 * 1024 * 1024),
        cost_estimate=pl.CostEstimate(
            flops=17_000_000_000, bytes_accessed=12_000_000, transcendentals=0
        ),
    )(*operands)
    return (results[0], results[1]) if first else (results[0], own)


def regroup_kernel(tm_count, inputs, me_ref, *refs):
    pieces, out_ref, stage, rows = refs[:-3], refs[-3], refs[-2], refs[-1]
    per = inputs // tm_count
    channels = out_ref.shape[0] // NSPEC
    for k in range(tm_count):
        source = me_ref[0] ^ k
        for plane in range(2):
            place = pl.ds(pl.multiple_of(plane * inputs + source * per, per), per)

            def fill(s, carry, piece=pieces[2 * k + plane], place=place):
                stage[s, place, :] = piece[s].astype(jnp.float32)
                return carry

            lax.fori_loop(0, NSPEC, fill, 0, unroll=5)

    def turn(s, carry):
        rows[pl.ds(s, channels, stride=NSPEC), :] = jnp.transpose(stage[s])
        return carry

    lax.fori_loop(0, NSPEC, turn, 0, unroll=5)
    out_ref[...] = rows[...].astype(jnp.bfloat16)


def regroup(pieces, me, inputs):
    tm_count = len(pieces)
    _, per, columns = pieces[0].shape
    channels = columns // 2
    block = min(LANES, channels)
    blocks = channels // block
    shape = (NSPEC, per, block)
    in_specs = [pl.BlockSpec(memory_space=pltpu.SMEM)]
    operands = [me]
    for piece in pieces:
        in_specs.append(pl.BlockSpec(shape, lambda c: (0, 0, c)))
        in_specs.append(pl.BlockSpec(shape, lambda c: (0, 0, blocks + c)))
        operands += [piece, piece]

    def kernel(*refs):
        regroup_kernel(tm_count, inputs, *refs)

    return pl.pallas_call(
        kernel,
        grid=(blocks,),
        out_shape=jax.ShapeDtypeStruct((channels * NSPEC, 2 * inputs), jnp.bfloat16),
        in_specs=in_specs,
        out_specs=pl.BlockSpec((block * NSPEC, 2 * inputs), lambda c: (c, 0)),
        scratch_shapes=[
            pltpu.VMEM((NSPEC, 2 * inputs, block), jnp.float32),
            pltpu.VMEM((block * NSPEC, 2 * inputs), jnp.float32),
        ],
        compiler_params=pltpu.CompilerParams(vmem_limit_bytes=40 * 1024 * 1024),
        cost_estimate=pl.CostEstimate(
            flops=4_000_000_000, bytes_accessed=4_000_000, transcendentals=0
        ),
    )(*operands)


def exchange(blocks, axis):
    count = lax.axis_size(axis)
    me = lax.axis_index(axis)
    pieces = [lax.dynamic_index_in_dim(blocks, me, 0, keepdims=False)]
    for k in range(1, count):
        block = lax.dynamic_index_in_dim(blocks, me ^ k, 0, keepdims=False)
        pieces.append(lax.ppermute(block, axis, [(d, d ^ k) for d in range(count)]))
    return pieces


def shards(voltages, taper):
    tm_count = lax.axis_size("tm")
    stat_count = lax.axis_size("stat")
    local_inputs, samples = voltages.shape
    frame_len = taper.shape[1]
    segment = frame_len // tm_count
    channel_count = frame_len // 2 // tm_count
    lag_count = stat_count // 2 + 1
    per = local_inputs // tm_count
    part_channels = channel_count // PARTS
    table = dft_table(segment, channel_count, frame_len, LANES)
    table = table.reshape(2 * segment, 2, PARTS, part_channels)
    me = lax.axis_index("tm").astype(jnp.int32).reshape(1)

    series = lax.all_to_all(
        voltages.reshape(tm_count, per, samples), "tm", split_axis=0, concat_axis=0, tiled=True
    )
    twisted = channelize(series, taper, LANES)
    twisted = twisted.reshape(tm_count * NSPEC * per, 2 * segment)
    blocks = []
    for part in range(PARTS):
        spectra = jnp.dot(
            twisted,
            table[:, :, part].reshape(2 * segment, 2 * part_channels),
            precision=lax.Precision.HIGH,
            preferred_element_type=jnp.float32,
        ).astype(jnp.bfloat16)
        spectra = spectra.reshape(tm_count, NSPEC, per, 2 * part_channels)
        blocks.append(regroup(exchange(spectra, "tm"), me, local_inputs))
    visibility = None
    own = [None] * PARTS
    for lag in range(lag_count):
        for part in range(PARTS):
            block = blocks[part]
            if lag < lag_count - 1:
                blocks[part] = from_behind(block, "stat", -1)
            visibility, own[part] = correlate(
                own[part], block, visibility, lag, lag_count, local_inputs, channel_count,
                part, PARTS,
            )
    return visibility[None]


def solution(mesh):
    return jax.shard_map(
        shards,
        mesh=mesh,
        in_specs=(P("stat", "tm"), P()),
        out_specs=P("tm", None, "stat", None, None, None),
        check_vma=False,
    )
```
